32 devices in a mesh: replica: 8 (over y, x, core), tensor: 4 (over z).
Axes of the slice: x: 2, y: 2, z: 4, core: 2. Of those that a mesh axis runs over, the one named last changes fastest.
Arguments:
- queries: bfloat16 [8, 128, 2, 8192], P('replica', None, None, 'tensor'), may hold values from -110 to 110
- step_key_value: bfloat16 [8, 128, 2, 2, 1024], P('replica', None, None, None, 'tensor'), may hold values from -4.1 to 4.1
- replica_page_store: bfloat16 [8, 2, 128, 64, 1024], P('replica', None, None, None, 'tensor'), may hold values from -4 to 4
- page_table: int32 [8, 128, 16], P('replica'), may hold values from 0 to 127
- lengths: int32 [8, 128], P('replica'), may hold values from 1 to 1024, 81920 in all within a row
- mig_offset: int32 [8, 14, 1], P('replica'), may hold values from 0 to 6; in each aligned block of 14 rows (0 to 13, 14 to 27, ..., all dimensions but the last counted through in order) at most 2 rows name the same one
- copy_order: int32 [8, 14, 16], P('replica'), may hold values from 0 to 15, each once within a row
- out_weight: bfloat16 [8192, 8192], P('tensor'), may hold values from -0.0625 to 0.0625
Outputs:
- attention: bfloat16 [8, 128, 2, 8192], P('replica', None, None, 'tensor')
- projected: bfloat16 [8, 128, 2, 8192], P('replica', 'tensor')
- arrived: bfloat16 [8, 14, 4, 2, 64, 1024], P('replica', None, None, None, None, 'tensor')
The draws below stay inside these ranges and needn't reach their ends.
Inputs may be any that keep to these rules, and one draw needn't show every extreme that they name: Row 114 + j of replica r arrived from replica (r + 1 + mig_offset[r, j, 0]) mod 8; at most 2 of one replica's arriving rows come from one source. `page_table`: entries name pages of the pool of the row's home replica; pages may be shared. `lengths`: each replica has a row of exactly 1024 tokens. `copy_order`: each row is an ordering of its 16 pages.
All inputs are finite; a program needn't handle non-finite values.
Results may differ from the reference program's by a relative error of at most 0.019.
Values may be sent and summed in bfloat16 or wider, within the bound.
A program may use at most 448 MiB of HBM per device.

```python
import math
import jax
import jax.numpy as jnp
import numpy as np
from jax import lax

D = 8192
QUERY_HEADS = 64
KEY_VALUE_HEADS = 8
HEAD_SIZE = 128
DECODE_ROWS = 128
MIGRANTS = 14
PAGE_TOKENS = 64
PAGES_ROW = 16
REPLICA_PAGES = 128
COPIED = 4
CAP = 2
N_REPLICA = 8


def draw_queries(key, part):
    key = jax.random.fold_in(key, 3)
    first_key = jax.random.fold_in(key, 0)
    value_rows = 2.0 * jnp.clip(jax.random.normal(first_key, (N_REPLICA, DECODE_ROWS, 2, QUERY_HEADS * HEAD_SIZE), jnp.float32), -4.0, 4.0)
    return value_rows.astype(jnp.bfloat16)


def draw_step_key_value(key, part):
    key = jax.random.fold_in(key, 7)
    value_rows = jnp.clip(jax.random.normal(key, (N_REPLICA, DECODE_ROWS, 2, 2, KEY_VALUE_HEADS * HEAD_SIZE), jnp.float32), -4.0, 4.0)
    return value_rows.astype(jnp.bfloat16)


def plant(result, stream_key, least, largest):
    longest = result.shape.index(max(result.shape))
    spots = []
    for shift in (0, 1):
        where = [jax.random.randint(jax.random.fold_in(stream_key, axis), (), 0, length) for axis, length in enumerate(result.shape)]
        where[longest] = (where[longest] + shift) % result.shape[longest]
        spots.append(tuple(where))
    return result.at[spots[0]].set(least).at[spots[1]].set(largest)


def block_scale(stream_key, shape, pieces, low, high):
    factor_of, own = 1.0, jax.random.fold_in(stream_key, 6)
    for dim, parts in pieces:
        draws = jnp.exp(jax.random.uniform(jax.random.fold_in(own, dim), (parts,), jnp.float32, low / len(pieces), high / len(pieces)))
        factor_of = factor_of * jnp.repeat(draws, shape[dim] // parts).reshape([-1 if axis == dim else 1 for axis in range(len(shape))])
    return factor_of


def profile(count, total, reach, skew):
    weights = [(1 << 20) // math.isqrt(rank ** skew) + 1 for rank in range(2, count + 1)]
    rest, given = total - reach - (count - 1), [1] * (count - 1)
    while rest > 0:
        candidates = [i for i in range(count - 1) if given[i] < reach]
        whole, remaining = sum([weights[i] for i in candidates]), rest
        for i in candidates:
            more = min(reach - given[i], max(1, remaining * weights[i] // whole), rest)
            given[i] = given[i] + more
            rest = rest - more
    return np.array([reach] + given)


def uneven_parts(stream_key, count, total, reach, slope):
    if count == 2:
        one = jax.random.randint(stream_key, (), max(1, total - reach), min(reach, total - 1) + 1)
        return jnp.stack([one, total - one])
    tallies = jnp.asarray(profile(count, total, reach, slope), jnp.int32)
    couples = (count - 1) // 2
    donor, sink = tallies[1:1 + 2 * couples:2], tallies[2:2 + 2 * couples:2]
    slack = jnp.minimum(donor - 1, reach - sink)
    passed = jax.random.randint(jax.random.fold_in(stream_key, 1), (couples,), 0, 1 << 20) % (slack + 1)
    tallies = tallies.at[1:1 + 2 * couples:2].set(donor - passed).at[2:2 + 2 * couples:2].set(sink + passed)
    return tallies[jax.random.permutation(jax.random.fold_in(stream_key, 2), count)]


def shared_out(key, own, number, rows, number_of, top, most, slope):
    ranking = jax.random.permutation(key, number_of)
    packed, usual = portions_of(number_of, rows * top, most, slope, True), portions_of(number_of, rows * top, most, slope, False)
    places = jnp.arange(number_of)

    def named(sizes, offset_by):
        used = int((sizes > 0).sum())
        fixed = max(1, used // 4)
        passed = fixed + (places - fixed + offset_by * (used - fixed)) % max(1, number_of - fixed)
        return jnp.zeros((number_of,), jnp.int32).at[ranking[jnp.where(places < fixed, places, passed)]].set(jnp.asarray(sizes, jnp.int32))

    sizes = jnp.where(number % 4 == 0, named(packed, number // 4), named(usual, number - number // 4 - 1))
    mixed = jax.random.permutation(jax.random.fold_in(own, 3), number_of)
    donor, sink = mixed[0:number_of // 2 * 2:2], mixed[1:number_of // 2 * 2:2]
    room = jnp.minimum(sizes[donor] - 1, most - sizes[sink]) // 2
    room = jnp.where((donor == ranking[0]) | (sink == ranking[0]) | (sizes[sink] == 0), 0, jnp.maximum(room, 0))
    passed = jax.random.randint(jax.random.fold_in(own, 4), (number_of // 2,), 0, 1 << 20) % (room + 1)
    sizes = sizes.at[donor].add(-passed).at[sink].add(passed)
    members = jnp.searchsorted(jnp.cumsum(sizes), jnp.arange(rows * top), side="right").astype(jnp.int32)
    table = members.reshape(top, rows).T
    table = table[jax.random.permutation(jax.random.fold_in(own, 1), rows)]
    offset_by = jax.random.randint(jax.random.fold_in(own, 2), (rows, 1), 0, top)
    return jnp.take_along_axis(table, (jnp.arange(top)[None, :] + offset_by) % top, axis=1)


def portions_of(count, total, limit, skew, full):
    portions = [(1 << 20) // math.isqrt(standing ** skew) + 1 for standing in range(1, count + 1)]
    largest = limit if full else min(limit, max(-(-total // count), total * portions[0] // sum(portions)))
    least = 1 if total - largest >= count - 1 else 0
    given, spare = [largest] + [least] * (count - 1), total - largest - least * (count - 1)
    while spare > 0:
        movable = [i for i in range(1, count) if given[i] < largest] or [i for i in range(1, count) if given[i] < limit]
        mass, budget = sum([portions[i] for i in movable]), spare
        for i in movable:
            extra = min(limit - given[i], max(1, budget * portions[i] // mass), spare)
            given[i] = given[i] + extra
            spare = spare - extra
    return np.array(given)


def noise(own_key, shape, spread, bound, cuts=(), kind=jnp.bfloat16):
    level = block_scale(own_key, shape, cuts, -0.22, 0.18) if cuts else 1.0
    values = jax.random.normal(own_key, shape, jnp.float32) * spread * level
    return jnp.minimum(jnp.maximum(values, -bound), bound).astype(kind)


def setup_inputs(seed: int = 0) -> dict:
    key_list = jax.random.split(jax.random.key(seed), 9)
    queries = draw_queries(jax.random.fold_in(key_list[8], 71), 0)
    step_key_value = draw_step_key_value(jax.random.fold_in(key_list[8], 71), 0)
    replica_page_store = noise(key_list[2], (N_REPLICA * 1, 2, REPLICA_PAGES, PAGE_TOKENS, KEY_VALUE_HEADS * HEAD_SIZE), 1.0, 4.0, ((0, 8), (4, 4)))
    page_table = plant(jax.random.randint(key_list[3], (N_REPLICA * 1, DECODE_ROWS, PAGES_ROW), 0, REPLICA_PAGES), jax.random.fold_in(key_list[3], 1), 0, REPLICA_PAGES - 1).astype(jnp.int32)
    lengths = jax.vmap(lambda own: uneven_parts(own, DECODE_ROWS, DECODE_ROWS * PAGES_ROW * PAGE_TOKENS * 5 // 8, PAGES_ROW * PAGE_TOKENS, 1))(jax.random.split(key_list[4], (N_REPLICA * 1))).reshape((N_REPLICA * 1, DECODE_ROWS)).astype(jnp.int32)
    mig_offset_keys = jax.random.split(jax.random.fold_in(key_list[5], 1), (N_REPLICA * 1) * MIGRANTS // MIGRANTS)
    mig_offset_turns = jax.random.permutation(jax.random.fold_in(key_list[5], 3), (N_REPLICA * 1) * MIGRANTS // MIGRANTS)
    mig_offset = jax.vmap(lambda own, number: shared_out(jax.random.fold_in(key_list[5], 2), own, number, MIGRANTS, N_REPLICA - 1, 1, CAP, 2))(mig_offset_keys, mig_offset_turns).reshape((N_REPLICA * 1, MIGRANTS, 1))
    copy_order = jax.vmap(lambda own: jax.random.permutation(own, PAGES_ROW))(jax.random.split(key_list[6], (N_REPLICA * 1) * MIGRANTS)).reshape((N_REPLICA * 1, MIGRANTS, PAGES_ROW)).astype(jnp.int32)
    out_weight = noise(key_list[7], (QUERY_HEADS * HEAD_SIZE, D), (QUERY_HEADS * HEAD_SIZE) ** -0.5, 0.0625, ((0, 4),))
    return dict(queries=queries, step_key_value=step_key_value, replica_page_store=replica_page_store, page_table=page_table, lengths=lengths, mig_offset=mig_offset, copy_order=copy_order, out_weight=out_weight)


NEG_FILL = -1e+30

def replica_rows(inputs, replica_page_store):
    queries, step_key_value, page_table, lengths, home_of = inputs
    query_group_size = QUERY_HEADS // KEY_VALUE_HEADS
    context_length = PAGES_ROW * PAGE_TOKENS
    selected_pages = replica_page_store[home_of[:, None], :, page_table]
    cached_page_keys = selected_pages[:, :, 0].reshape(DECODE_ROWS, context_length, KEY_VALUE_HEADS, HEAD_SIZE)
    cached_page_values = selected_pages[:, :, 1].reshape(DECODE_ROWS, context_length, KEY_VALUE_HEADS, HEAD_SIZE)
    fresh_token = step_key_value.reshape(DECODE_ROWS, 2, 2, KEY_VALUE_HEADS, HEAD_SIZE)
    all_keys = jnp.concatenate([cached_page_keys, fresh_token[:, :, 0]], axis=1).astype(jnp.float32)
    all_values = jnp.concatenate([cached_page_values, fresh_token[:, :, 1]], axis=1).astype(jnp.float32)
    query_head_vectors = queries.reshape(DECODE_ROWS, 2, KEY_VALUE_HEADS, query_group_size, HEAD_SIZE).astype(jnp.float32)
    scores = jnp.einsum('rsgjd,rkgd->rsgjk', query_head_vectors, all_keys, precision=lax.Precision.HIGHEST) / math.sqrt(HEAD_SIZE)
    position = jnp.arange(context_length + 2, dtype=jnp.int32)
    step_index = jnp.arange(2, dtype=jnp.int32)
    allowed = jnp.where(position[None, None, :] < context_length, position[None, None, :] < lengths[:, None, None], position[None, None, :] - context_length <= step_index[None, :, None])
    allowed = allowed[:, :, None, None, :]
    masked = jnp.where(allowed, scores, NEG_FILL)
    highest = lax.optimization_barrier(jnp.max(masked, axis=-1, keepdims=True))
    weights = jnp.where(allowed, jnp.exp(masked - highest), 0.0).astype(jnp.bfloat16)
    weights = lax.optimization_barrier(weights).astype(jnp.float32)
    total = lax.optimization_barrier(jnp.sum(weights, axis=-1))
    weighted = jnp.einsum('rsgjk,rkgd->rsgjd', weights, all_values, precision=lax.Precision.HIGHEST)
    return (weighted / total[..., None]).astype(jnp.bfloat16).reshape(DECODE_ROWS, 2, QUERY_HEADS * HEAD_SIZE)

def reference(queries, step_key_value, replica_page_store, page_table, lengths, mig_offset, copy_order, out_weight):
    replica_ids = jnp.arange(N_REPLICA, dtype=jnp.int32)
    source_of = (replica_ids[:, None] + 1 + mig_offset[:, :, 0]) % N_REPLICA
    home_of = jnp.concatenate([jnp.broadcast_to(replica_ids[:, None], (N_REPLICA, DECODE_ROWS - MIGRANTS)), source_of], axis=1)
    attention = lax.map(lambda inputs: replica_rows(inputs, replica_page_store), (queries, step_key_value, page_table, lengths, home_of))
    projected = jnp.dot(attention.reshape(-1, QUERY_HEADS * HEAD_SIZE), out_weight, preferred_element_type=jnp.float32)
    projected = projected.astype(jnp.bfloat16).reshape(N_REPLICA, DECODE_ROWS, 2, D)
    wanted = jnp.take_along_axis(page_table[:, DECODE_ROWS - MIGRANTS:], copy_order[:, :, :COPIED], axis=2)
    arrived = replica_page_store[source_of[:, :, None], :, wanted]
    return (attention, projected, arrived)
```

```python
import functools
import math

import jax
import jax.numpy as jnp
from jax import lax
from jax.experimental import pallas as pl
from jax.experimental.pallas import tpu as pltpu
from jax.sharding import PartitionSpec as P

HEAD_SIZE = 128
MIGRANTS = 14
COPIED = 4
CHUNKS = 4
NEG_FILL = -1e30


def attend_rows(rows, kv_heads, group, pages, page_len, table, lengths, queries, fresh, pool, out):
    context = pages * page_len
    scale = math.log2(math.e) / math.sqrt(HEAD_SIZE)
    height = kv_heads * 2 * group
    position = lax.broadcasted_iota(jnp.int32, (1, context), 1)
    step = lax.broadcasted_iota(jnp.int32, (height, 1), 0) // group % 2
    scores, news = [], []
    for row in rows:
        q = queries[0, row]
        keys = jnp.concatenate([pool[0, 0, table[row, i]] for i in range(pages)], axis=0)
        scores.append(
            lax.dot_general(q, keys, (((1,), (1,)), ((), ())), preferred_element_type=jnp.float32)
        )
        wide = q.astype(jnp.float32)
        token = fresh[0, row]
        first = jnp.sum(wide * token[0:1], axis=1, keepdims=True) * scale
        second = jnp.sum(wide * token[2:3], axis=1, keepdims=True) * scale
        news.append((first, jnp.where(step > 0, second, NEG_FILL)))
    parts = []
    for row, s, (first, second) in zip(rows, scores, news):
        s = jnp.where(position < lengths[row], s * scale, NEG_FILL)
        highest = jnp.maximum(jnp.max(s, axis=1, keepdims=True), jnp.maximum(first, second))
        weights = jnp.exp2(s - highest)
        first = jnp.exp2(first - highest)
        second = jnp.exp2(second - highest)
        total = jnp.sum(weights, axis=1, keepdims=True) + first + second
        parts.append((weights.astype(jnp.bfloat16), first, second, total))
    for row, (weights, first, second, total) in zip(rows, parts):
        values = jnp.concatenate([pool[0, 1, table[row, i]] for i in range(pages)], axis=0)
        weighted = jnp.dot(weights, values, preferred_element_type=jnp.float32)
        token = fresh[0, row]
        weighted = weighted + first * token[1:2] + second * token[3:4]
        weighted = weighted / total
        for g in range(kv_heads):
            block = weighted[g * 2 * group : (g + 1) * 2 * group, g * HEAD_SIZE : (g + 1) * HEAD_SIZE]
            out[row, g * 2 * group : (g + 1) * 2 * group] = block.astype(jnp.bfloat16)


def chunk_kernel(
    sizes, unroll, row_of, staying, table, lengths, queries, fresh, pool, out
):
    def step(index, carry):
        base = index * unroll

        @pl.when(row_of(base) < staying)
        def _():
            attend_rows(
                [base + k for k in range(unroll)], *sizes, table, lengths, queries, fresh, pool, out
            )

        return carry

    lax.fori_loop(0, out.shape[0] // unroll, step, 0)


def slot_kernel(sizes, unroll, table, lengths, wanted, queries, fresh, pool, out, copied):
    def copy(row, carry):
        for c in range(COPIED):
            copied[row, c, 0] = pool[0, 0, wanted[row, c]]
            copied[row, c, 1] = pool[0, 1, wanted[row, c]]
        return carry

    lax.fori_loop(0, out.shape[0], copy, 0)

    def step(index, carry):
        attend_rows(
            [index * unroll + k for k in range(unroll)],
            *sizes, table, lengths, queries, fresh, pool, out
        )
        return carry

    lax.fori_loop(0, out.shape[0] // unroll, step, 0)


def unroll_of(count):
    return next(u for u in (4, 2, 1) if count % u == 0)


def body(
    queries,
    step_key_value,
    replica_page_store,
    page_table,
    lengths,
    mig_offset,
    copy_order,
    out_weight,
):
    replicas = lax.axis_size("replica")
    shards = lax.axis_size("tensor")
    own_index = lax.axis_index("replica")
    capacity = max(2, (MIGRANTS + replicas - 2) // (replicas - 1))
    slots = replicas * capacity
    row_count = queries.shape[1]
    width = queries.shape[-1]
    kv_width = step_key_value.shape[-1]
    kv_heads = kv_width // HEAD_SIZE
    group = width // HEAD_SIZE // kv_heads
    height = kv_heads * 2 * group
    staying = row_count - MIGRANTS
    pages = page_table.shape[-1]
    page_len = replica_page_store.shape[3]
    per_shard = row_count // shards
    share = per_shard // CHUNKS
    chunk_rows = share * shards
    sizes = (kv_heads, group, pages, page_len)

    def spread(q):
        q = q.reshape(-1, 2, kv_heads, group, HEAD_SIZE).transpose(0, 2, 1, 3, 4)
        same = jnp.eye(kv_heads, dtype=jnp.bool_)[None, :, None, None, :, None]
        q = jnp.where(same, q[:, :, :, :, None, :], jnp.zeros((), q.dtype))
        return q.reshape(-1, height, kv_width)

    def gathered(att):
        att = att.reshape(-1, kv_heads, 2, group, HEAD_SIZE).transpose(0, 2, 1, 3, 4)
        return att.reshape(-1, 2, width)

    def by_chunk(x):
        x = x.reshape((shards, CHUNKS, share) + x.shape[1:])
        x = jnp.moveaxis(x, 1, 0)
        return x.reshape((CHUNKS, chunk_rows) + x.shape[3:])

    source_of = (own_index + 1 + mig_offset[0, :, 0]) % replicas
    earlier = lax.broadcasted_iota(jnp.int32, (MIGRANTS, MIGRANTS), 0) > lax.broadcasted_iota(
        jnp.int32, (MIGRANTS, MIGRANTS), 1
    )
    same_source = source_of[:, None] == source_of[None, :]
    slot_rank = jnp.sum(jnp.where(earlier & same_source, 1, 0), axis=1)
    slot_of = source_of * capacity + slot_rank
    placing = lax.broadcasted_iota(jnp.int32, (slots, MIGRANTS), 0) == slot_of[None, :]
    mig_table = page_table[0, staying:]
    mig_wanted = jnp.take_along_axis(mig_table, copy_order[0, :, :COPIED], axis=1)
    mig_ints = jnp.concatenate(
        [mig_table, mig_wanted, lengths[0, staying:, None]], axis=1
    )
    send_ints = jnp.sum(jnp.where(placing[:, :, None], mig_ints[None], 0), axis=1)
    mig_rows = jnp.concatenate(
        [
            queries[0, staying:].reshape(MIGRANTS, -1),
            step_key_value[0, staying:].reshape(MIGRANTS, -1),
        ],
        axis=1,
    )
    place = placing.astype(jnp.bfloat16)
    send_rows = jnp.dot(place, mig_rows, preferred_element_type=jnp.float32).astype(jnp.bfloat16)
    got_ints = lax.all_to_all(
        send_ints.reshape(replicas, capacity, -1), "replica", 0, 0, tiled=True
    ).reshape(slots, -1)
    got_rows = lax.all_to_all(
        send_rows.reshape(replicas, capacity, -1), "replica", 0, 0, tiled=True
    ).reshape(slots, -1)

    smem = pl.BlockSpec(memory_space=pltpu.SMEM)
    vmem = pl.BlockSpec(memory_space=pltpu.VMEM)
    params = pltpu.CompilerParams(vmem_limit_bytes=40 * 2**20)

    slot_cost = pl.CostEstimate(
        flops=4 * slots * height * pages * page_len * kv_width,
        bytes_accessed=12 * 2**20,
        transcendentals=slots * height * pages * page_len,
    )
    slot_att, sending = pl.pallas_call(
        functools.partial(slot_kernel, sizes, unroll_of(slots)),
        out_shape=(
            jax.ShapeDtypeStruct((slots, height, HEAD_SIZE), jnp.bfloat16),
            jax.ShapeDtypeStruct((slots, COPIED, 2, page_len, kv_width), jnp.bfloat16),
        ),
        in_specs=[smem, smem, smem, vmem, vmem, vmem],
        out_specs=(vmem, vmem),
        compiler_params=params,
        cost_estimate=slot_cost,
        name="slot_attention",
    )(
        got_ints[:, :pages],
        got_ints[:, pages + COPIED],
        got_ints[:, pages : pages + COPIED],
        spread(got_rows[:, : 2 * width].reshape(slots, 2, width))[None],
        got_rows[:, 2 * width :].astype(jnp.float32).reshape(1, slots, 4, kv_width),
        replica_page_store,
    )
    incoming = lax.all_to_all(
        sending.reshape((replicas, capacity) + sending.shape[1:]), "replica", 0, 0, tiled=True
    ).reshape(sending.shape)
    arrived = jnp.take(incoming, slot_of, axis=0, mode="clip")
    back = lax.all_to_all(
        gathered(slot_att).reshape(replicas, capacity, -1), "replica", 0, 0, tiled=True
    ).reshape(slots, -1)
    mig_att = (
        jnp.dot(place.T, back, preferred_element_type=jnp.float32)
        .astype(jnp.bfloat16)
        .reshape(MIGRANTS, 2, width)
    )

    all_queries = by_chunk(spread(queries[0]))
    all_fresh = by_chunk(step_key_value[0].astype(jnp.float32).reshape(row_count, 4, kv_width))
    all_table = by_chunk(page_table[0])
    all_lengths = by_chunk(lengths[0])
    chunk_cost = pl.CostEstimate(
        flops=4 * chunk_rows * height * pages * page_len * kv_width,
        bytes_accessed=9 * 2**20,
        transcendentals=chunk_rows * height * pages * page_len,
    )
    unroll = unroll_of(share)
    attention, projected = [], []
    for c in range(CHUNKS):

        def row_of(j, c=c):
            return j // share * per_shard + c * share + j % share

        att = pl.pallas_call(
            functools.partial(chunk_kernel, sizes, unroll, row_of, staying),
            grid=(1,),
            out_shape=jax.ShapeDtypeStruct((chunk_rows, height, HEAD_SIZE), jnp.bfloat16),
            in_specs=[
                smem,
                smem,
                pl.BlockSpec((1, chunk_rows, height, kv_width), lambda i, c=c: (c, 0, 0, 0)),
                pl.BlockSpec((1, chunk_rows, 4, kv_width), lambda i, c=c: (c, 0, 0, 0)),
                vmem,
            ],
            out_specs=vmem,
            compiler_params=params,
            cost_estimate=chunk_cost,
            name="chunk_attention",
        )(all_table[c], all_lengths[c], all_queries, all_fresh, replica_page_store)
        att = gathered(att)
        for t in range(shards):
            low = t * per_shard + c * share
            first = max(low, staying)
            if first < low + share:
                at = t * share + first - low
                piece = mig_att[first - staying : low + share - staying]
                att = lax.dynamic_update_slice(att, piece, (at, 0, 0))
        attention.append(att)
        product = jnp.dot(
            att.reshape(chunk_rows * 2, width), out_weight, preferred_element_type=jnp.float32
        ).astype(jnp.bfloat16)
        if projected:
            product, projected[-1] = lax.optimization_barrier((product, projected[-1]))
        projected.append(lax.psum_scatter(product, "tensor", scatter_dimension=0, tiled=True))
    attention = jnp.stack([a.reshape(shards, share, 2, width) for a in attention], axis=1)
    attention = attention.reshape(1, row_count, 2, width)
    projected = jnp.concatenate(projected, axis=0).reshape(per_shard, 2, -1)
    return (attention, projected[None], arrived[None])


def solution(mesh):
    placed = (
        P("replica", None, None, "tensor"),
        P("replica", None, None, None, "tensor"),
        P("replica", None, None, None, "tensor"),
        P("replica", None, None),
        P("replica", None),
        P("replica", None, None),
        P("replica", None, None),
        P("tensor", None),
    )
    return jax.shard_map(
        body,
        mesh=mesh,
        in_specs=placed,
        out_specs=(
            P("replica", None, None, "tensor"),
            P("replica", "tensor", None, None),
            P("replica", None, None, None, None, "tensor"),
        ),
        check_vma=False,
    )
```

```python
import functools
import math

import jax
import jax.numpy as jnp
from jax import lax
from jax.experimental import pallas as pl
from jax.experimental.pallas import tpu as pltpu
from jax.sharding import PartitionSpec as P

HEAD_SIZE = 128
MIGRANTS = 14
COPIED = 4
CHUNKS = 2
DIGIT = 128
TILE = 512
NEG_FILL = -1e30


def attend_rows(rows, kv_heads, group, pages, page_len, table, lengths, queries, fresh, pool, out):
    context = pages * page_len
    scale = math.log2(math.e) / math.sqrt(HEAD_SIZE)
    height = kv_heads * 2 * group
    position = lax.broadcasted_iota(jnp.int32, (1, context), 1)
    step = lax.broadcasted_iota(jnp.int32, (height, 1), 0) // group % 2
    scores, news = [], []
    for row in rows:
        q = queries[0, row]
        keys = jnp.concatenate([pool[0, 0, table[row, i]] for i in range(pages)], axis=0)
        scores.append(
            lax.dot_general(q, keys, (((1,), (1,)), ((), ())), preferred_element_type=jnp.float32)
        )
        wide = q.astype(jnp.float32)
        token = fresh[0, row]
        first = jnp.sum(wide * token[0:1], axis=1, keepdims=True) * scale
        second = jnp.sum(wide * token[2:3], axis=1, keepdims=True) * scale
        news.append((first, jnp.where(step > 0, second, NEG_FILL)))
    parts = []
    for row, s, (first, second) in zip(rows, scores, news):
        s = jnp.where(position < lengths[row], s * scale, NEG_FILL)
        highest = jnp.maximum(jnp.max(s, axis=1, keepdims=True), jnp.maximum(first, second))
        weights = jnp.exp2(s - highest)
        first = jnp.exp2(first - highest)
        second = jnp.exp2(second - highest)
        total = jnp.sum(weights, axis=1, keepdims=True) + first + second
        parts.append((weights.astype(jnp.bfloat16), first, second, total))
    for row, (weights, first, second, total) in zip(rows, parts):
        values = jnp.concatenate([pool[0, 1, table[row, i]] for i in range(pages)], axis=0)
        weighted = jnp.dot(weights, values, preferred_element_type=jnp.float32)
        token = fresh[0, row]
        weighted = weighted + first * token[1:2] + second * token[3:4]
        weighted = weighted / total
        for g in range(kv_heads):
            block = weighted[g * 2 * group : (g + 1) * 2 * group, g * HEAD_SIZE : (g + 1) * HEAD_SIZE]
            out[row, g * 2 * group : (g + 1) * 2 * group] = block.astype(jnp.bfloat16)


def chunk_kernel(
    sizes, unroll, row_of, staying, table, lengths, queries, fresh, pool, out
):
    def step(index, carry):
        base = index * unroll

        @pl.when(row_of(base) < staying)
        def _():
            attend_rows(
                [base + k for k in range(unroll)], *sizes, table, lengths, queries, fresh, pool, out
            )

        return carry

    lax.fori_loop(0, out.shape[0] // unroll, step, 0)


def slot_kernel(sizes, unroll, table, lengths, wanted, queries, fresh, pool, out, copied):
    def copy(row, carry):
        for c in range(COPIED):
            copied[row, c, 0] = pool[0, 0, wanted[row, c]]
            copied[row, c, 1] = pool[0, 1, wanted[row, c]]
        return carry

    lax.fori_loop(0, out.shape[0], copy, 0)

    def step(index, carry):
        attend_rows(
            [index * unroll + k for k in range(unroll)],
            *sizes, table, lengths, queries, fresh, pool, out
        )
        return carry

    lax.fori_loop(0, out.shape[0] // unroll, step, 0)


def project_kernel(rows, weight, out):
    out[...] = jnp.dot(
        rows[...], weight[...], preferred_element_type=jnp.float32
    ).astype(out.dtype)


def project(rows, weight):
    count, depth = rows.shape
    columns = weight.shape[1]
    tile = math.gcd(columns, TILE)
    return pl.pallas_call(
        project_kernel,
        grid=(columns // tile,),
        out_shape=jax.ShapeDtypeStruct((count, columns), rows.dtype),
        in_specs=[
            pl.BlockSpec((count, depth), lambda i: (0, 0)),
            pl.BlockSpec((depth, tile), lambda i: (0, i)),
        ],
        out_specs=pl.BlockSpec((count, tile), lambda i: (0, i)),
        compiler_params=pltpu.CompilerParams(vmem_limit_bytes=24 * 2**20),
        cost_estimate=pl.CostEstimate(
            flops=2 * count * depth * columns,
            bytes_accessed=2 * (depth * columns + count * (depth + columns)),
            transcendentals=0,
        ),
        name="project",
    )(rows, weight)


def unroll_of(count):
    return next(u for u in (4, 2, 1) if count % u == 0)


def body(
    queries,
    step_key_value,
    replica_page_store,
    page_table,
    lengths,
    mig_offset,
    copy_order,
    out_weight,
):
    replicas = lax.axis_size("replica")
    shards = lax.axis_size("tensor")
    own_index = lax.axis_index("replica")
    capacity = max(2, (MIGRANTS + replicas - 2) // (replicas - 1))
    slots = replicas * capacity
    row_count = queries.shape[1]
    width = queries.shape[-1]
    kv_width = step_key_value.shape[-1]
    kv_heads = kv_width // HEAD_SIZE
    group = width // HEAD_SIZE // kv_heads
    height = kv_heads * 2 * group
    staying = row_count - MIGRANTS
    pages = page_table.shape[-1]
    page_len = replica_page_store.shape[3]
    per_shard = row_count // shards
    share = per_shard // CHUNKS
    chunk_rows = share * shards
    sizes = (kv_heads, group, pages, page_len)

    def spread(q):
        q = q.reshape(-1, 2, kv_heads, group, HEAD_SIZE).transpose(0, 2, 1, 3, 4)
        same = jnp.eye(kv_heads, dtype=jnp.bool_)[None, :, None, None, :, None]
        q = jnp.where(same, q[:, :, :, :, None, :], jnp.zeros((), q.dtype))
        return q.reshape(-1, height, kv_width)

    def gathered(att):
        att = att.reshape(-1, kv_heads, 2, group, HEAD_SIZE).transpose(0, 2, 1, 3, 4)
        return att.reshape(-1, 2, width)

    def by_chunk(x):
        x = x.reshape((shards, CHUNKS, share) + x.shape[1:])
        x = jnp.moveaxis(x, 1, 0)
        return x.reshape((CHUNKS, chunk_rows) + x.shape[3:])

    source_of = (own_index + 1 + mig_offset[0, :, 0]) % replicas
    earlier = lax.broadcasted_iota(jnp.int32, (MIGRANTS, MIGRANTS), 0) > lax.broadcasted_iota(
        jnp.int32, (MIGRANTS, MIGRANTS), 1
    )
    same_source = source_of[:, None] == source_of[None, :]
    slot_rank = jnp.sum(jnp.where(earlier & same_source, 1, 0), axis=1)
    slot_of = source_of * capacity + slot_rank
    placing = lax.broadcasted_iota(jnp.int32, (slots, MIGRANTS), 0) == slot_of[None, :]
    mig_table = page_table[0, staying:]
    mig_wanted = jnp.take_along_axis(mig_table, copy_order[0, :, :COPIED], axis=1)
    mig_ints = jnp.concatenate(
        [mig_table, mig_wanted, lengths[0, staying:, None]], axis=1
    )
    ints = mig_ints.shape[1]
    mig_rows = jnp.concatenate(
        [
            queries[0, staying:].reshape(MIGRANTS, -1),
            step_key_value[0, staying:].reshape(MIGRANTS, -1),
            (mig_ints // DIGIT).astype(jnp.bfloat16),
            (mig_ints % DIGIT).astype(jnp.bfloat16),
            jnp.zeros((MIGRANTS, -2 * ints % 128), jnp.bfloat16),
        ],
        axis=1,
    )
    place = placing.astype(jnp.bfloat16)
    send_rows = jnp.dot(place, mig_rows, preferred_element_type=jnp.float32).astype(jnp.bfloat16)
    got_rows = lax.all_to_all(
        send_rows.reshape(replicas, capacity, -1), "replica", 0, 0, tiled=True
    ).reshape(slots, -1)

    tail = 2 * width + 4 * kv_width
    digits = got_rows[:, tail : tail + 2 * ints].astype(jnp.int32)
    got_ints = digits[:, :ints] * DIGIT + digits[:, ints:]

    smem = pl.BlockSpec(memory_space=pltpu.SMEM)
    vmem = pl.BlockSpec(memory_space=pltpu.VMEM)
    params = pltpu.CompilerParams(vmem_limit_bytes=28 * 2**20)

    slot_cost = pl.CostEstimate(
        flops=4 * slots * height * pages * page_len * kv_width,
        bytes_accessed=12 * 2**20,
        transcendentals=slots * height * pages * page_len,
    )
    slot_att, sending = pl.pallas_call(
        functools.partial(slot_kernel, sizes, unroll_of(slots)),
        out_shape=(
            jax.ShapeDtypeStruct((slots, height, HEAD_SIZE), jnp.bfloat16),
            jax.ShapeDtypeStruct((slots, COPIED, 2, page_len, kv_width), jnp.bfloat16),
        ),
        in_specs=[smem, smem, smem, vmem, vmem, vmem],
        out_specs=(vmem, vmem),
        compiler_params=params,
        cost_estimate=slot_cost,
        name="slot_attention",
    )(
        got_ints[:, :pages],
        got_ints[:, pages + COPIED],
        got_ints[:, pages : pages + COPIED],
        spread(got_rows[:, : 2 * width].reshape(slots, 2, width))[None],
        got_rows[:, 2 * width : tail].astype(jnp.float32).reshape(1, slots, 4, kv_width),
        replica_page_store,
    )
    incoming = lax.all_to_all(
        sending.reshape((replicas, capacity) + sending.shape[1:]), "replica", 0, 0, tiled=True
    ).reshape(sending.shape)
    arrived = jnp.take(incoming, slot_of, axis=0, mode="clip")
    back = lax.all_to_all(
        gathered(slot_att).reshape(replicas, capacity, -1), "replica", 0, 0, tiled=True
    ).reshape(slots, -1)
    mig_att = (
        jnp.dot(place.T, back, preferred_element_type=jnp.float32)
        .astype(jnp.bfloat16)
        .reshape(MIGRANTS, 2, width)
    )

    all_queries = by_chunk(spread(queries[0]))
    all_fresh = by_chunk(step_key_value[0].astype(jnp.float32).reshape(row_count, 4, kv_width))
    all_table = by_chunk(page_table[0])
    all_lengths = by_chunk(lengths[0])
    chunk_cost = pl.CostEstimate(
        flops=4 * chunk_rows * height * pages * page_len * kv_width,
        bytes_accessed=9 * 2**20,
        transcendentals=chunk_rows * height * pages * page_len,
    )
    unroll = unroll_of(share)
    attention, projected = [], []
    for c in range(CHUNKS):

        def row_of(j, c=c):
            return j // share * per_shard + c * share + j % share

        att = pl.pallas_call(
            functools.partial(chunk_kernel, sizes, unroll, row_of, staying),
            grid=(1,),
            out_shape=jax.ShapeDtypeStruct((chunk_rows, height, HEAD_SIZE), jnp.bfloat16),
            in_specs=[
                smem,
                smem,
                pl.BlockSpec((1, chunk_rows, height, kv_width), lambda i, c=c: (c, 0, 0, 0)),
                pl.BlockSpec((1, chunk_rows, 4, kv_width), lambda i, c=c: (c, 0, 0, 0)),
                vmem,
            ],
            out_specs=vmem,
            compiler_params=params,
            cost_estimate=chunk_cost,
            name="chunk_attention",
        )(all_table[c], all_lengths[c], all_queries, all_fresh, replica_page_store)
        att = gathered(att)
        for t in range(shards):
            low = t * per_shard + c * share
            first = max(low, staying)
            if first < low + share:
                at = t * share + first - low
                piece = mig_att[first - staying : low + share - staying]
                att = lax.dynamic_update_slice(att, piece, (at, 0, 0))
        attention.append(att)
        product = project(att.reshape(chunk_rows * 2, width), out_weight)
        if projected:
            product, projected[-1] = lax.optimization_barrier((product, projected[-1]))
        projected.append(lax.psum_scatter(product, "tensor", scatter_dimension=0, tiled=True))
    attention = jnp.stack([a.reshape(shards, share, 2, width) for a in attention], axis=1)
    attention = attention.reshape(1, row_count, 2, width)
    projected = jnp.concatenate(projected, axis=0).reshape(per_shard, 2, -1)
    return (attention, projected[None], arrived[None])


def solution(mesh):
    placed = (
        P("replica", None, None, "tensor"),
        P("replica", None, None, None, "tensor"),
        P("replica", None, None, None, "tensor"),
        P("replica", None, None),
        P("replica", None),
        P("replica", None, None),
        P("replica", None, None),
        P("tensor", None),
    )
    return jax.shard_map(
        body,
        mesh=mesh,
        in_specs=placed,
        out_specs=(
            P("replica", None, None, "tensor"),
            P("replica", "tensor", None, None),
            P("replica", None, None, None, None, "tensor"),
        ),
        check_vma=False,
    )
```

```python
import functools
import math

import jax
import jax.numpy as jnp
from jax import lax
from jax.experimental import pallas as pl
from jax.experimental.pallas import tpu as pltpu
from jax.sharding import PartitionSpec as P

HEAD_SIZE = 128
MIGRANTS = 14
COPIED = 4
CHUNKS = 2
DIGIT = 128
NEG_FILL = -1e30


def attend_rows(rows, kv_heads, group, pages, page_len, table, lengths, queries, fresh, pool, out):
    context = pages * page_len
    scale = math.log2(math.e) / math.sqrt(HEAD_SIZE)
    height = kv_heads * 2 * group
    position = lax.broadcasted_iota(jnp.int32, (1, context), 1)
    step = lax.broadcasted_iota(jnp.int32, (height, 1), 0) // group % 2
    scores, news = [], []
    for row in rows:
        q = queries[0, row]
        keys = jnp.concatenate([pool[0, 0, table[row, i]] for i in range(pages)], axis=0)
        scores.append(
            lax.dot_general(q, keys, (((1,), (1,)), ((), ())), preferred_element_type=jnp.float32)
        )
        wide = q.astype(jnp.float32)
        token = fresh[0, row]
        first = jnp.sum(wide * token[0:1], axis=1, keepdims=True) * scale
        second = jnp.sum(wide * token[2:3], axis=1, keepdims=True) * scale
        news.append((first, jnp.where(step > 0, second, NEG_FILL)))
    parts = []
    for row, s, (first, second) in zip(rows, scores, news):
        s = jnp.where(position < lengths[row], s * scale, NEG_FILL)
        highest = jnp.maximum(jnp.max(s, axis=1, keepdims=True), jnp.maximum(first, second))
        weights = jnp.exp2(s - highest)
        first = jnp.exp2(first - highest)
        second = jnp.exp2(second - highest)
        total = jnp.sum(weights, axis=1, keepdims=True) + first + second
        parts.append((weights.astype(jnp.bfloat16), first, second, total))
    for row, (weights, first, second, total) in zip(rows, parts):
        values = jnp.concatenate([pool[0, 1, table[row, i]] for i in range(pages)], axis=0)
        weighted = jnp.dot(weights, values, preferred_element_type=jnp.float32)
        token = fresh[0, row]
        weighted = weighted + first * token[1:2] + second * token[3:4]
        weighted = weighted / total
        for g in range(kv_heads):
            block = weighted[g * 2 * group : (g + 1) * 2 * group, g * HEAD_SIZE : (g + 1) * HEAD_SIZE]
            out[row, g * 2 * group : (g + 1) * 2 * group] = block.astype(jnp.bfloat16)


def chunk_kernel(
    sizes, unroll, row_of, staying, table, lengths, queries, fresh, pool, out
):
    def step(index, carry):
        base = index * unroll

        @pl.when(row_of(base) < staying)
        def _():
            attend_rows(
                [base + k for k in range(unroll)], *sizes, table, lengths, queries, fresh, pool, out
            )

        return carry

    lax.fori_loop(0, out.shape[0] // unroll, step, 0)


def slot_kernel(sizes, unroll, table, lengths, wanted, queries, fresh, pool, out, copied):
    def copy(row, carry):
        for c in range(COPIED):
            copied[row, c, 0] = pool[0, 0, wanted[row, c]]
            copied[row, c, 1] = pool[0, 1, wanted[row, c]]
        return carry

    lax.fori_loop(0, out.shape[0], copy, 0)

    def step(index, carry):
        attend_rows(
            [index * unroll + k for k in range(unroll)],
            *sizes, table, lengths, queries, fresh, pool, out
        )
        return carry

    lax.fori_loop(0, out.shape[0] // unroll, step, 0)


def unroll_of(count):
    return next(u for u in (4, 2, 1) if count % u == 0)


def body(
    queries,
    step_key_value,
    replica_page_store,
    page_table,
    lengths,
    mig_offset,
    copy_order,
    out_weight,
):
    replicas = lax.axis_size("replica")
    shards = lax.axis_size("tensor")
    own_index = lax.axis_index("replica")
    capacity = max(2, (MIGRANTS + replicas - 2) // (replicas - 1))
    slots = replicas * capacity
    row_count = queries.shape[1]
    width = queries.shape[-1]
    kv_width = step_key_value.shape[-1]
    kv_heads = kv_width // HEAD_SIZE
    group = width // HEAD_SIZE // kv_heads
    height = kv_heads * 2 * group
    staying = row_count - MIGRANTS
    pages = page_table.shape[-1]
    page_len = replica_page_store.shape[3]
    per_shard = row_count // shards
    share = per_shard // CHUNKS
    chunk_rows = share * shards
    sizes = (kv_heads, group, pages, page_len)

    def spread(q):
        q = q.reshape(-1, 2, kv_heads, group, HEAD_SIZE).transpose(0, 2, 1, 3, 4)
        same = jnp.eye(kv_heads, dtype=jnp.bool_)[None, :, None, None, :, None]
        q = jnp.where(same, q[:, :, :, :, None, :], jnp.zeros((), q.dtype))
        return q.reshape(-1, height, kv_width)

    def gathered(att):
        att = att.reshape(-1, kv_heads, 2, group, HEAD_SIZE).transpose(0, 2, 1, 3, 4)
        return att.reshape(-1, 2, width)

    def by_chunk(x):
        x = x.reshape((shards, CHUNKS, share) + x.shape[1:])
        x = jnp.moveaxis(x, 1, 0)
        return x.reshape((CHUNKS, chunk_rows) + x.shape[3:])

    source_of = (own_index + 1 + mig_offset[0, :, 0]) % replicas
    earlier = lax.broadcasted_iota(jnp.int32, (MIGRANTS, MIGRANTS), 0) > lax.broadcasted_iota(
        jnp.int32, (MIGRANTS, MIGRANTS), 1
    )
    same_source = source_of[:, None] == source_of[None, :]
    slot_rank = jnp.sum(jnp.where(earlier & same_source, 1, 0), axis=1)
    slot_of = source_of * capacity + slot_rank
    placing = lax.broadcasted_iota(jnp.int32, (slots, MIGRANTS), 0) == slot_of[None, :]
    mig_table = page_table[0, staying:]
    mig_wanted = jnp.take_along_axis(mig_table, copy_order[0, :, :COPIED], axis=1)
    mig_ints = jnp.concatenate(
        [mig_table, mig_wanted, lengths[0, staying:, None]], axis=1
    )
    ints = mig_ints.shape[1]
    mig_rows = jnp.concatenate(
        [
            queries[0, staying:].reshape(MIGRANTS, -1),
            step_key_value[0, staying:].reshape(MIGRANTS, -1),
            (mig_ints // DIGIT).astype(jnp.bfloat16),
            (mig_ints % DIGIT).astype(jnp.bfloat16),
            jnp.zeros((MIGRANTS, -2 * ints % 128), jnp.bfloat16),
        ],
        axis=1,
    )
    place = placing.astype(jnp.bfloat16)
    send_rows = jnp.dot(place, mig_rows, preferred_element_type=jnp.float32).astype(jnp.bfloat16)
    got_rows = lax.all_to_all(
        send_rows.reshape(replicas, capacity, -1), "replica", 0, 0, tiled=True
    ).reshape(slots, -1)

    tail = 2 * width + 4 * kv_width
    digits = got_rows[:, tail : tail + 2 * ints].astype(jnp.int32)
    got_ints = digits[:, :ints] * DIGIT + digits[:, ints:]

    smem = pl.BlockSpec(memory_space=pltpu.SMEM)
    vmem = pl.BlockSpec(memory_space=pltpu.VMEM)
    params = pltpu.CompilerParams(vmem_limit_bytes=28 * 2**20)

    slot_cost = pl.CostEstimate(
        flops=4 * slots * height * pages * page_len * kv_width,
        bytes_accessed=12 * 2**20,
        transcendentals=slots * height * pages * page_len,
    )
    slot_att, sending = pl.pallas_call(
        functools.partial(slot_kernel, sizes, unroll_of(slots)),
        out_shape=(
            jax.ShapeDtypeStruct((slots, height, HEAD_SIZE), jnp.bfloat16),
            jax.ShapeDtypeStruct((slots, COPIED, 2, page_len, kv_width), jnp.bfloat16),
        ),
        in_specs=[smem, smem, smem, vmem, vmem, vmem],
        out_specs=(vmem, vmem),
        compiler_params=params,
        cost_estimate=slot_cost,
        name="slot_attention",
    )(
        got_ints[:, :pages],
        got_ints[:, pages + COPIED],
        got_ints[:, pages : pages + COPIED],
        spread(got_rows[:, : 2 * width].reshape(slots, 2, width))[None],
        got_rows[:, 2 * width : tail].astype(jnp.float32).reshape(1, slots, 4, kv_width),
        replica_page_store,
    )
    slot_att, sending, moved_table = lax.optimization_barrier((slot_att, sending, page_table[0]))
    all_table = by_chunk(moved_table)
    incoming = lax.all_to_all(
        sending.reshape((replicas, capacity) + sending.shape[1:]), "replica", 0, 0, tiled=True
    ).reshape(sending.shape)
    back = lax.all_to_all(
        gathered(slot_att).reshape(replicas, capacity, -1), "replica", 0, 0, tiled=True
    ).reshape(slots, -1)
    mig_att = (
        jnp.dot(place.T, back, preferred_element_type=jnp.float32)
        .astype(jnp.bfloat16)
        .reshape(MIGRANTS, 2, width)
    )

    all_queries = by_chunk(spread(queries[0]))
    all_fresh = by_chunk(step_key_value[0].astype(jnp.float32).reshape(row_count, 4, kv_width))
    all_lengths = by_chunk(lengths[0])
    chunk_cost = pl.CostEstimate(
        flops=4 * chunk_rows * height * pages * page_len * kv_width,
        bytes_accessed=9 * 2**20,
        transcendentals=chunk_rows * height * pages * page_len,
    )
    unroll = unroll_of(share)
    attention, projected = [], []
    for c in range(CHUNKS):

        def row_of(j, c=c):
            return j // share * per_shard + c * share + j % share

        att = pl.pallas_call(
            functools.partial(chunk_kernel, sizes, unroll, row_of, staying),
            grid=(1,),
            out_shape=jax.ShapeDtypeStruct((chunk_rows, height, HEAD_SIZE), jnp.bfloat16),
            in_specs=[
                smem,
                smem,
                pl.BlockSpec((1, chunk_rows, height, kv_width), lambda i, c=c: (c, 0, 0, 0)),
                pl.BlockSpec((1, chunk_rows, 4, kv_width), lambda i, c=c: (c, 0, 0, 0)),
                vmem,
            ],
            out_specs=vmem,
            compiler_params=params,
            cost_estimate=chunk_cost,
            name="chunk_attention",
        )(all_table[c], all_lengths[c], all_queries, all_fresh, replica_page_store)
        att = gathered(att)
        for t in range(shards):
            low = t * per_shard + c * share
            first = max(low, staying)
            if first < low + share:
                at = t * share + first - low
                piece = mig_att[first - staying : low + share - staying]
                att = lax.dynamic_update_slice(att, piece, (at, 0, 0))
        attention.append(att)
        if c == CHUNKS - 1:
            att, incoming = lax.optimization_barrier((att, incoming))
        product = jnp.dot(
            att.reshape(chunk_rows * 2, width), out_weight, preferred_element_type=jnp.float32
        ).astype(jnp.bfloat16)
        if projected:
            product, projected[-1] = lax.optimization_barrier((product, projected[-1]))
        projected.append(lax.psum_scatter(product, "tensor", scatter_dimension=0, tiled=True))
    arrived = jnp.take(incoming, slot_of, axis=0, mode="clip")
    attention = jnp.stack([a.reshape(shards, share, 2, width) for a in attention], axis=1)
    attention = attention.reshape(1, row_count, 2, width)
    projected = jnp.concatenate(projected, axis=0).reshape(per_shard, 2, -1)
    return (attention, projected[None], arrived[None])


def solution(mesh):
    placed = (
        P("replica", None, None, "tensor"),
        P("replica", None, None, None, "tensor"),
        P("replica", None, None, None, "tensor"),
        P("replica", None, None),
        P("replica", None),
        P("replica", None, None),
        P("replica", None, None),
        P("tensor", None),
    )
    return jax.shard_map(
        body,
        mesh=mesh,
        in_specs=placed,
        out_specs=(
            P("replica", None, None, "tensor"),
            P("replica", "tensor", None, None),
            P("replica", None, None, None, None, "tensor"),
        ),
        check_vma=False,
    )
```
